32 devices in a mesh: row: 4 (over z), col: 4 (over y, core), front: 2 (over x).
Axes of the slice: x: 2, y: 2, z: 4, core: 2. Of those that a mesh axis runs over, the one named last changes fastest.
Arguments:
- front: float32 [2, 12, 1024, 12, 1024], P('front', None, 'row', None, 'col')
- child_update: float32 [2, 2048, 2048], P('front', 'row', 'col'), may hold values from -6 to 6
- child_map: int32 [2, 2048], P('front'), may hold values from 0 to 12287, as said below
- pattern: int32 [2, 48, 48], P('front'), may hold values 0 or 1
Outputs:
- new_front: float32 [2, 12, 1024, 12, 1024], P('front', None, 'row', None, 'col')
The draws below stay inside these ranges and needn't reach their ends.
Inputs may be any that keep to these rules, and one draw needn't show every extreme that they name: `child_map`: entries of one front are distinct. Each aligned run of 512 entries holds exactly 128 entries g with (g // 256) % 4 equal to each index of col.
All inputs are finite; a program needn't handle non-finite values. No bound on the sum of `pattern` on one device may be relied on, other than what follows from the above.
Results may differ from the reference program's by a relative error of at most 0.0001.
Values sent between devices are 32-bit elements; how exact they have to be, the bound alone decides.
A program may use at most 320 MiB of HBM per device.

```python
import jax
import jax.numpy as jnp
from jax import lax

NF = 12288
BS = 256
PB = 4
NC = 2048
PW = 1024
NB = 48
LR = 12
LC = 12
N_ROW = 4
N_COL = 4


def draw_front(key, part):
    key = jax.random.fold_in(key, 1)
    key_values = jax.random.fold_in(key, 0)
    values = jax.random.normal(key_values, (2, NF, NF), jnp.float32)
    places = jnp.arange(NF, dtype=jnp.int32)
    diagonal = (places[:, None] == places[None, :]).astype(jnp.float32)
    values = values + 8.0 * PW ** 0.5 * diagonal[None]
    return values.reshape(2, LR, N_ROW * BS, LC, N_COL * BS)


def one_child_map(key):
    per_owner = NC // N_COL
    per_slab = NC // (N_COL * N_COL)
    owner_cols = NF // N_COL
    keys = jax.random.split(key, 2 * N_COL)
    chosen = jax.vmap(lambda sub_key: jax.random.permutation(sub_key, owner_cols)[:per_owner])(keys[:N_COL])
    owners = jnp.arange(N_COL, dtype=jnp.int32)[:, None]
    placed = (chosen // BS * N_COL + owners) * BS + chosen % BS
    placed = placed.reshape(N_COL, N_COL, per_slab).transpose(1, 0, 2).reshape(N_COL, N_COL * per_slab)
    shuffles = jax.vmap(lambda sub_key: jax.random.permutation(sub_key, N_COL * per_slab))(keys[N_COL:])
    placed = jnp.take_along_axis(placed, shuffles.astype(jnp.int32), axis=1)
    return placed.reshape(NC).astype(jnp.int32)


def draw_child_map(key, part):
    key = jax.random.fold_in(key, 2)
    keys = jax.random.split(key, 2)
    return jax.vmap(one_child_map)(keys)


def place_ends(drawn, stream_key, least, largest):
    dims = drawn.shape
    place = [jax.random.randint(jax.random.fold_in(stream_key, axis), (), 0, dims[axis]) for axis in range(len(dims))]
    drawn = drawn.at[tuple(place)].set(least)
    longest = dims.index(max(dims))
    place[longest] = (place[longest] + 1) % dims[longest]
    return drawn.at[tuple(place)].set(largest)


def level_of(rng, dims, shards, smallest, largest):
    loudness, own = 1.0, jax.random.fold_in(rng, 6)
    for position, parts in shards:
        steps = jnp.exp(jax.random.uniform(jax.random.fold_in(own, position), (parts,), jnp.float32, smallest / len(shards), largest / len(shards)))
        loudness = loudness * jnp.repeat(steps, dims[position] // parts).reshape([-1 if axis == position else 1 for axis in range(len(dims))])
    return loudness


def centred(rng, shape, deviation, reach, cuts=(), kind=jnp.bfloat16):
    entries = deviation * jax.random.normal(rng, shape, jnp.float32)
    if cuts:
        entries = entries * level_of(rng, shape, cuts, -0.22, 0.18)
    return jnp.clip(entries, -reach, reach).astype(kind)


def setup_inputs(seed: int = 0) -> dict:
    streams_of = jax.random.split(jax.random.key(seed), 5)
    front = draw_front(jax.random.fold_in(streams_of[4], 71), 0)
    child_update = centred(streams_of[1], (2, NC, NC), 1.0, 6.0, ((0, 2), (1, 4), (2, 4)), jnp.float32)
    child_map = draw_child_map(jax.random.fold_in(streams_of[4], 71), 0)
    pattern = place_ends((jax.random.randint(streams_of[3], (2, NB, NB), 0, 2) < 1).astype(jnp.int32), jax.random.fold_in(streams_of[3], 1), 0, 1)
    return dict(front=front, child_update=child_update, child_map=child_map, pattern=pattern)


def one_front(front_tile, update, mapping, blocks_kept):
    full = front_tile.reshape(NF, NF)
    added = full.at[mapping[:, None], mapping[None, :]].add(update)
    corner = added[:PW, :PW]
    factor = jnp.linalg.cholesky(0.5 * (corner + corner.T))
    identity = jnp.eye(PW, dtype=jnp.float32)
    inverse = jax.scipy.linalg.solve_triangular(factor, identity, lower=True)
    panel = jnp.dot(added[:, :PW], inverse.T, precision=lax.Precision.HIGHEST)
    schur = jnp.dot(panel, panel.T, precision=lax.Precision.HIGHEST)
    trailing = jnp.arange(NB) >= PB
    chosen = ((blocks_kept == 1) & trailing[:, None] & trailing[None, :]).astype(jnp.float32)
    result = added.reshape(NB, BS, NB, BS) - schur.reshape(NB, BS, NB, BS) * chosen[:, None, :, None]
    result = result.reshape(NF, NF)
    result = result.at[:, :PW].set(panel)
    return result.reshape(LR, N_ROW * BS, LC, N_COL * BS)

def reference(front, child_update, child_map, pattern):
    results = []
    for which in range(2):
        results.append(one_front(front[which], child_update[which], child_map[which], pattern[which]))
    return jnp.stack(results, axis=0)
```

```python
import functools

import jax
import jax.numpy as jnp
from jax import lax
from jax.experimental import pallas as pl
from jax.experimental.pallas import tpu as pltpu
from jax.sharding import PartitionSpec as P

PB = 4
PW = 1024
DB = 128


def broadcast(value, axis, source):
    kept = jnp.where(lax.axis_index(axis) == source, value, 0).astype(value.dtype)
    return lax.psum(kept, axis)


def exact_dot(left, right):
    return jnp.dot(left, right, precision=lax.Precision.HIGHEST, preferred_element_type=jnp.float32)


def factor_inverse_kernel(corner_ref, high_ref, low_ref, inv_ref, work_ref, diag_ref, unit_ref):
    work_ref[...] = corner_ref[...]
    inv_ref[...] = jnp.zeros_like(inv_ref)
    lanes = lax.broadcasted_iota(jnp.int32, (DB, DB), 1)
    rows = lax.broadcasted_iota(jnp.int32, (DB, DB), 0)
    quarter = DB // 4
    for start in range(0, PW, DB):
        stop = start + DB
        diag_ref[...] = work_ref[start:stop, start:stop]
        unit_ref[...] = (lanes == rows).astype(jnp.float32)
        for first in range(0, DB, quarter):
            lane_ids = lanes[first:]
            row_ids = rows[first:]

            def eliminate(place, carry):
                pivot_row = diag_ref[pl.ds(place, 1), :]
                unit_row = unit_ref[pl.ds(place, 1), :]
                lower = diag_ref[first:, :]
                pivot = jnp.sum(jnp.where(lanes[:1] == place, pivot_row, 0.0), axis=1, keepdims=True)
                column = jnp.sum(jnp.where(lane_ids == place, lower, 0.0), axis=1, keepdims=True)
                scale = jnp.where(row_ids > place, column * (1.0 / pivot), 0.0)
                diag_ref[first:, :] = lower - scale * pivot_row
                unit_ref[first:, :] = unit_ref[first:, :] - scale * unit_row
                return carry

            lax.fori_loop(first, first + quarter, eliminate, 0)
        pivots = jnp.sum(jnp.where(lanes == rows, diag_ref[...], 0.0), axis=1, keepdims=True)
        block_inverse = unit_ref[...] / jnp.sqrt(pivots)
        inv_ref[start:stop, start:stop] = block_inverse
        if start:
            inv_ref[start:stop, :start] = exact_dot(block_inverse, inv_ref[start:stop, :start])
        if stop < PW:
            upper = exact_dot(block_inverse, work_ref[start:stop, stop:])
            below = upper.T
            work_ref[stop:, stop:] = work_ref[stop:, stop:] - exact_dot(below, upper)
            inv_ref[stop:, :stop] = inv_ref[stop:, :stop] - exact_dot(below, inv_ref[start:stop, :stop])
    high_ref[...], low_ref[...] = split_two(inv_ref[...])


def factor_inverse(corner):
    return pl.pallas_call(
        factor_inverse_kernel,
        out_shape=[jax.ShapeDtypeStruct((PW, PW), jnp.bfloat16)] * 2,
        in_specs=[pl.BlockSpec(memory_space=pltpu.VMEM)],
        out_specs=[pl.BlockSpec(memory_space=pltpu.VMEM)] * 2,
        scratch_shapes=[
            pltpu.VMEM((PW, PW), jnp.float32),
            pltpu.VMEM((PW, PW), jnp.float32),
            pltpu.VMEM((DB, DB), jnp.float32),
            pltpu.VMEM((DB, DB), jnp.float32),
        ],
        compiler_params=pltpu.CompilerParams(vmem_limit_bytes=48 * 1024 * 1024),
        cost_estimate=pl.CostEstimate(flops=100_000_000_000, bytes_accessed=8 * PW * PW, transcendentals=0),
        name="factor_inverse",
    )(corner)


def split_two(value):
    high = value.astype(jnp.bfloat16)
    low = (value - high.astype(jnp.float32)).astype(jnp.bfloat16)
    return high, low


def matmul(left, right):
    return jnp.dot(left, right, preferred_element_type=jnp.float32)


def matmul_nt(left, right):
    return lax.dot_general(left, right, (((1,), (1,)), ((), ())), preferred_element_type=jnp.float32)


def place_kernel(front_ref, rows_ref, hits_ref, out_ref):
    values = rows_ref[...]
    high = values.astype(jnp.bfloat16)
    rest = values - high.astype(jnp.float32)
    middle, low = split_two(rest)
    block_size = out_ref.shape[-1]
    for m in range(out_ref.shape[2]):
        hits = hits_ref[:, m * block_size:(m + 1) * block_size]
        added = matmul(low, hits) + matmul(middle, hits) + matmul(high, hits)
        out_ref[0, 0, m] = front_ref[0, 0, m] + added


def place_children(front, placed_rows, col_hits):
    _, local_rows, local_cols, block_size, _ = front.shape
    count = placed_rows.shape[1]
    spec = pl.BlockSpec((1, 1, local_cols, block_size, block_size), lambda i: (0, i, 0, 0, 0))
    return pl.pallas_call(
        place_kernel,
        grid=(local_rows,),
        out_shape=jax.ShapeDtypeStruct(front.shape, jnp.float32),
        in_specs=[
            spec,
            pl.BlockSpec((block_size, count), lambda i: (i, 0)),
            pl.BlockSpec(col_hits.shape, lambda i: (0, 0)),
        ],
        out_specs=spec,
        compiler_params=pltpu.CompilerParams(vmem_limit_bytes=40 * 1024 * 1024),
        cost_estimate=pl.CostEstimate(
            flops=6 * front.size * count, bytes_accessed=8 * front.size, transcendentals=0
        ),
        name="place_children",
    )(front, placed_rows, col_hits)


def solve_kernel(split, raw_ref, high_ref, low_ref, *out_refs):
    block_size = raw_ref.shape[-1]
    pieces = [split_two(raw_ref[k]) for k in range(PB)]
    for n in range(PB):
        total = None
        for k in range(n + 1):
            raw_high, raw_low = pieces[k]
            here = (slice(n * block_size, (n + 1) * block_size), slice(k * block_size, (k + 1) * block_size))
            inv_high, inv_low = high_ref[here], low_ref[here]
            term = matmul_nt(raw_low, inv_high) + matmul_nt(raw_high, inv_low) + matmul_nt(raw_high, inv_high)
            total = term if total is None else total + term
        columns = slice(n * block_size, (n + 1) * block_size)
        if split:
            out_refs[0][:, columns], out_refs[1][:, columns] = split_two(total)
        else:
            out_refs[0][:, columns] = total


def solve_rows(raw, inv_high, inv_low, split):
    parts, rows, block_size = raw.shape
    out_spec = pl.BlockSpec((block_size, PW), lambda i: (i, 0))
    if split:
        out_shape = [jax.ShapeDtypeStruct((rows, PW), jnp.bfloat16)] * 2
    else:
        out_shape = [jax.ShapeDtypeStruct((rows, PW), jnp.float32)]
    whole = pl.BlockSpec((PW, PW), lambda i: (0, 0))
    return pl.pallas_call(
        functools.partial(solve_kernel, split),
        grid=(rows // block_size,),
        out_shape=out_shape,
        in_specs=[pl.BlockSpec((parts, block_size, block_size), lambda i: (0, i, 0)), whole, whole],
        out_specs=[out_spec] * len(out_shape),
        compiler_params=pltpu.CompilerParams(vmem_limit_bytes=40 * 1024 * 1024),
        cost_estimate=pl.CostEstimate(
            flops=4 * rows * PW * PW, bytes_accessed=8 * rows * PW, transcendentals=0
        ),
        name="solve_rows",
    )(raw, inv_high, inv_low)


def schur_kernel(kept_ref, own_ref, sum_ref, solved_ref, high_ref, low_ref, out_ref):
    i = pl.program_id(0)
    block_size = out_ref.shape[-1]
    solved_high, solved_low = split_two(solved_ref[...])
    for m in range(out_ref.shape[2]):
        rows = slice(m * block_size, (m + 1) * block_size)
        kept = kept_ref[i, m] == 1

        @pl.when(kept)
        def _():
            high, low = high_ref[rows, :], low_ref[rows, :]
            product = matmul_nt(solved_low, high) + matmul_nt(solved_high, low) + matmul_nt(solved_high, high)
            out_ref[0, 0, m] = sum_ref[0, 0, m] - product

        @pl.when(jnp.logical_not(kept))
        def _():
            out_ref[0, 0, m] = sum_ref[0, 0, m]

    @pl.when(own_ref[0] < PB)
    def _():
        place = pl.multiple_of(jnp.minimum(own_ref[0], PB - 1) * block_size, block_size)
        out_ref[0, 0, 0] = solved_ref[:, pl.ds(place, block_size)]


def schur_update(kept, own, summed, solved, col_high, col_low):
    _, local_rows, local_cols, block_size, _ = summed.shape
    spec = pl.BlockSpec((1, 1, local_cols, block_size, block_size), lambda i, *_: (0, i, 0, 0, 0))
    whole = pl.BlockSpec(
        col_high.shape, lambda i, *_: (0, 0), pipeline_mode=pl.Buffered(buffer_count=1)
    )
    return pl.pallas_call(
        schur_kernel,
        out_shape=jax.ShapeDtypeStruct(summed.shape, jnp.float32),
        grid_spec=pltpu.PrefetchScalarGridSpec(
            num_scalar_prefetch=2,
            grid=(local_rows,),
            in_specs=[spec, pl.BlockSpec((block_size, PW), lambda i, *_: (i, 0)), whole, whole],
            out_specs=spec,
        ),
        input_output_aliases={2: 0},
        compiler_params=pltpu.CompilerParams(vmem_limit_bytes=52 * 1024 * 1024),
        cost_estimate=pl.CostEstimate(
            flops=6 * summed.size * PW, bytes_accessed=8 * summed.size, transcendentals=0
        ),
        name="schur_update",
    )(kept, own, summed, solved, col_high, col_low)


def per_device(front, child_update, child_map, pattern):
    rows_count = lax.axis_size("row")
    cols_count = lax.axis_size("col")
    row_place = lax.axis_index("row")
    col_place = lax.axis_index("col")
    blocks = front.transpose(0, 1, 3, 2, 4)
    local_rows, local_cols, block_size = blocks.shape[1:4]
    update = child_update[0]
    slab_rows, slab_cols = update.shape
    per_row = slab_rows // rows_count
    per_col = slab_cols // cols_count
    targets = child_map[0]
    target_block = targets // block_size
    target_within = targets % block_size
    target_row = target_block // rows_count * block_size + target_within
    target_col = target_block // cols_count * block_size + target_within
    row_order = jnp.argsort(
        (target_block % rows_count).reshape(rows_count, slab_rows), axis=1, stable=True
    )
    row_order = (
        row_order + (jnp.arange(rows_count, dtype=jnp.int32) * slab_rows)[:, None]
    ).reshape(rows_count, rows_count, per_row)
    col_order = jnp.argsort(
        (target_block % cols_count).reshape(cols_count, slab_cols), axis=1, stable=True
    )
    col_order = (
        col_order + (jnp.arange(cols_count, dtype=jnp.int32) * slab_cols)[:, None]
    ).reshape(cols_count, cols_count, per_col)
    send_rows = (jnp.take(row_order, row_place, axis=0) - row_place * slab_rows).reshape(-1)
    send_cols = (jnp.take(col_order, col_place, axis=0) - col_place * slab_cols).reshape(-1)
    recv_rows = target_row[jnp.take(row_order, row_place, axis=1).reshape(-1)]
    recv_cols = target_col[jnp.take(col_order, col_place, axis=1).reshape(-1)]
    outgoing = update[send_rows][:, send_cols].reshape(rows_count, per_row, cols_count, per_col)
    outgoing = outgoing.transpose(0, 2, 1, 3).reshape(rows_count * cols_count, per_row * per_col)
    landed = lax.all_to_all(outgoing, ("row", "col"), split_axis=0, concat_axis=0, tiled=True)
    landed = landed.reshape(rows_count, cols_count, per_row, per_col).transpose(0, 2, 1, 3)
    landed = landed.reshape(rows_count * per_row, cols_count * per_col)
    row_places = jnp.arange(local_rows * block_size, dtype=jnp.int32)
    col_places = jnp.arange(local_cols * block_size, dtype=jnp.int32)
    row_hits = (row_places[:, None] == recv_rows[None, :]).astype(jnp.float32)
    col_hits = (recv_cols[:, None] == col_places[None, :]).astype(jnp.float32)
    placed_rows = jnp.dot(row_hits, landed, precision=lax.Precision.HIGHEST)
    leading = blocks[0, :, 0].reshape(local_rows * block_size, block_size)
    leading = leading + jnp.dot(
        placed_rows, col_hits[:, :block_size], precision=lax.Precision.HIGHEST
    )
    square = rows_count == cols_count == PB
    if square:
        corner = lax.all_gather(leading[:block_size], "row", axis=0, tiled=True)
        corner = lax.all_gather(corner, "col", axis=1, tiled=True)
        corner, leading = lax.optimization_barrier((corner, leading))
        panel_raw = lax.all_gather(leading, "col", axis=0, tiled=False)
        swap = [
            (p * cols_count + q, q * cols_count + p)
            for p in range(rows_count)
            for q in range(cols_count)
        ]
        swapped = lax.ppermute(leading, ("row", "col"), swap)
        column_raw = lax.all_gather(swapped, "row", axis=0, tiled=False)
    else:
        panel_parts = []
        for root_col in range(PB):
            panel_parts.append(broadcast(leading, "col", root_col))
        panel_raw = jnp.stack(panel_parts)
        upper_rows = jnp.concatenate([part[:block_size] for part in panel_parts], axis=1)
        corner = lax.all_gather(upper_rows, "row", axis=0, tiled=True)[:PW]
        selected = (
            jnp.arange(local_cols, dtype=jnp.int32) * (cols_count // rows_count)
            + col_place // rows_count
        )
        candidate = panel_raw.reshape(PB, local_rows, block_size, block_size)[:, selected]
        candidate = candidate.reshape(PB, local_cols * block_size, block_size)
        column_raw = broadcast(candidate, "row", col_place % rows_count)
    summed = place_children(blocks, placed_rows, col_hits.astype(jnp.bfloat16))
    inv_high, inv_low = factor_inverse(0.5 * (corner + corner.T))
    (solved,) = solve_rows(panel_raw, inv_high, inv_low, False)
    col_high, col_low = solve_rows(column_raw, inv_high, inv_low, True)
    block_rows = jnp.arange(local_rows, dtype=jnp.int32) * rows_count + row_place
    block_cols = jnp.arange(local_cols, dtype=jnp.int32) * cols_count + col_place
    pattern_here = pattern[0][block_rows[:, None], block_cols[None, :]]
    applied = (
        (pattern_here == 1) & (block_rows[:, None] >= PB) & (block_cols[None, :] >= PB)
    ).astype(jnp.int32)
    own = jnp.full((1,), col_place, jnp.int32)
    result = schur_update(applied, own, summed, solved, col_high, col_low)
    return result.transpose(0, 1, 3, 2, 4)


def solution(mesh):
    placed = (
        P("front", None, "row", None, "col"),
        P("front", "row", "col"),
        P("front", None),
        P("front", None, None),
    )
    return jax.shard_map(
        per_device,
        mesh=mesh,
        in_specs=placed,
        out_specs=P("front", None, "row", None, "col"),
        check_vma=False,
    )
```
